32 devices in a mesh: seq: 8 (over z, x), head: 4 (over y, core).
Axes of the slice: x: 2, y: 2, z: 4, core: 2. Of those that a mesh axis runs over, the one named last changes fastest.
Arguments:
- queries: bfloat16 [2048, 2048], P('seq', 'head'), may hold values from -30 to 30, as said below
- keys: bfloat16 [2048, 2048], P('seq', 'head'), may hold values from -30 to 30, as said below
- values: bfloat16 [2048, 2048], P('seq', 'head'), may hold values from -6 to 6
- out_grad: bfloat16 [2048, 2048], P('seq', 'head'), may hold values from -6 to 6
- rand_blocks: int32 [16, 16, 3], P('head', 'seq'), may hold values from 0 to 15, as said below
Outputs:
- attn_out: bfloat16 [2048, 2048], P('seq', 'head')
- grad_queries: bfloat16 [2048, 2048], P('seq', 'head')
- grad_keys: bfloat16 [2048, 2048], P('seq', 'head')
- grad_values: bfloat16 [2048, 2048], P('seq', 'head')
The draws below stay inside these ranges and needn't reach their ends.
Inputs may be any that keep to these rules, and one draw needn't show every extreme that they name: queries are of order one; in some draws a few rows reach larger scales. keys are of order one; in some draws a few rows reach larger scales. `rand_blocks`: for each aligned group of 4 heads and each aligned run of 2 query blocks, at most 3 of the group's entries name blocks of one aligned run of 2 key blocks, and in every group some run is named exactly 3 times.
All inputs are finite; a program needn't handle non-finite values.
Results may differ from the reference program's by a relative error of at most 0.015.
The reference program's roundings to bfloat16 on the way count: a program that leaves them out, or rounds other values in their place, can miss the bound.
Values may be sent and summed in bfloat16 or wider, within the bound.
A program may use at most 192 MiB of HBM per device.

```python
import math
import jax
import jax.numpy as jnp
from jax import lax

HEADS = 16
DH = 128
BS = 128
RAND = 3
BLK_DEV = 2
NB = 16
SEQ = 2048
HL = 4
CAP = 3
NEAR_BITS = 1
FAR_BITS = 3


def base_pair(key):
    row_count = NB * BS
    row_width = HEADS * DH
    query_base = jnp.clip(jax.random.normal(jax.random.fold_in(key, 11), (row_count, row_width), jnp.float32), -6.0, 6.0)
    key_base = jnp.clip(jax.random.normal(jax.random.fold_in(key, 12), (row_count, row_width), jnp.float32), -6.0, 6.0)
    return (query_base, key_base)


def draw_queries(key, part):
    query_base, key_base = base_pair(key)
    result = query_base
    return result.astype(jnp.bfloat16)


def draw_keys(key, part):
    query_base, key_base = base_pair(key)
    result = key_base
    return result.astype(jnp.bfloat16)


def draw_rand_blocks(key, part):
    seq_groups = NB // BLK_DEV
    head_groups = HEADS // HL
    per_group = HL * BLK_DEV * RAND
    hot_devs = jax.random.permutation(jax.random.fold_in(key, 21), seq_groups) < max(1, seq_groups // 8)

    def one_group(group_key):
        owner_order = jax.random.permutation(jax.random.fold_in(group_key, 1), seq_groups)
        hot_rank = jnp.argsort(jnp.where(hot_devs[owner_order], 0, 1).astype(jnp.int32), stable=True)
        owner_order = owner_order[hot_rank]
        owner_list = jnp.repeat(owner_order, CAP, total_repeat_length=seq_groups * CAP)[:per_group]
        owner_list = owner_list[jax.random.permutation(jax.random.fold_in(group_key, 2), per_group)]
        local_blk = jax.random.randint(jax.random.fold_in(group_key, 3), (per_group,), 0, BLK_DEV)
        return owner_list * BLK_DEV + local_blk
    group_keys = jax.random.split(jax.random.fold_in(key, 20), head_groups * seq_groups)
    flat_ids = jax.vmap(one_group)(group_keys)
    arranged = flat_ids.reshape(head_groups, seq_groups, HL, BLK_DEV, RAND).transpose(0, 2, 1, 3, 4)
    return arranged.reshape(HEADS, NB, RAND).astype(jnp.int32)


def block_levels(stream_key, dims, shards, smallest, top_value):
    def one(axis_at, parts):
        draws = jax.random.uniform(jax.random.fold_in(jax.random.fold_in(stream_key, 6), axis_at), (parts,), jnp.float32, smallest / len(shards), top_value / len(shards))
        return jnp.repeat(jnp.exp(draws), dims[axis_at] // parts).reshape((-1,) + (1,) * (len(dims) - axis_at - 1))

    loudness = one(*shards[0])
    for cut in shards[1:]:
        loudness = loudness * one(*cut)
    return loudness


def normal_values(key, extent, width, limit, pieces=(), held_as=jnp.bfloat16):
    values = width * jax.random.normal(key, extent, jnp.float32)
    if pieces:
        values = values * block_levels(key, extent, pieces, -0.22, 0.18)
    return jnp.clip(values, -limit, limit).astype(held_as)


def setup_inputs(seed: int = 0) -> dict:
    seeds = jax.random.split(jax.random.key(seed), 6)
    queries = draw_queries(jax.random.fold_in(seeds[5], 71), 0)
    keys = draw_keys(jax.random.fold_in(seeds[5], 71), 0)
    values = normal_values(seeds[2], (SEQ, HEADS * DH), 1.0, 6.0, ((0, 8), (1, 4)))
    out_grad = normal_values(seeds[3], (SEQ, HEADS * DH), 1.0, 6.0, ((0, 8), (1, 4)))
    rand_blocks = draw_rand_blocks(jax.random.fold_in(seeds[5], 71), 0)
    return {"queries": queries, "keys": keys, "values": values, "out_grad": out_grad, "rand_blocks": rand_blocks}


def round_trip(value_arr):
    return lax.optimization_barrier(value_arr.astype(jnp.bfloat16)).astype(jnp.float32)

def reference(queries, keys, values, out_grad, rand_blocks):
    score_scale = 1.0 / math.sqrt(DH)
    bit_count = NEAR_BITS + FAR_BITS
    block_ids = jnp.arange(NB, dtype=jnp.int32)
    fixed_cols = [block_ids] + [jnp.bitwise_xor(block_ids, jnp.int32(1 << bit_pos)) for bit_pos in range(bit_count)]
    fixed_index = jnp.stack(fixed_cols, axis=1)

    def by_head(array_in):
        return array_in.reshape(NB, BS, HEADS, DH).transpose(2, 0, 1, 3)

    def one_head(head_items):
        query_rows, key_rows, value_rows, grad_rows, rand_rows = head_items
        key_index = jnp.concatenate([fixed_index, rand_rows.astype(jnp.int32)], axis=1)
        key_set = key_rows[key_index].astype(jnp.float32)
        value_set = value_rows[key_index].astype(jnp.float32)
        query_wide = query_rows.astype(jnp.float32)
        grad_wide = grad_rows.astype(jnp.float32)
        scores = jnp.einsum('btd,bksd->btks', query_wide, key_set) * score_scale
        row_max = lax.optimization_barrier(jnp.max(scores, axis=(2, 3)))
        log_total = row_max + jnp.log(lax.optimization_barrier(jnp.sum(jnp.exp(scores - row_max[:, :, None, None]), axis=(2, 3))))
        weights = jnp.exp(scores - log_total[:, :, None, None])
        weights_low = round_trip(weights)
        attn_rows = jnp.einsum('btks,bksd->btd', weights_low, value_set).astype(jnp.bfloat16)
        attn_wide = lax.optimization_barrier(attn_rows).astype(jnp.float32)
        row_delta = lax.optimization_barrier(jnp.sum(grad_wide * attn_wide, axis=2))
        grad_weights = jnp.einsum('btd,bksd->btks', grad_wide, value_set)
        grad_scores = round_trip(weights * (grad_weights - row_delta[:, :, None, None]))
        grad_query = (score_scale * jnp.einsum('btks,bksd->btd', grad_scores, key_set)).astype(jnp.bfloat16)
        key_terms = score_scale * jnp.einsum('btks,btd->bksd', grad_scores, query_wide)
        value_terms = jnp.einsum('btks,btd->bksd', weights_low, grad_wide)
        zero_rows = jnp.zeros((NB, BS, DH), jnp.float32)
        grad_key = key_terms[:, 0] + zero_rows.at[key_index[:, 1:]].add(round_trip(key_terms[:, 1:]))
        grad_value = value_terms[:, 0] + zero_rows.at[key_index[:, 1:]].add(round_trip(value_terms[:, 1:]))
        return (attn_rows, grad_query, grad_key.astype(jnp.bfloat16), grad_value.astype(jnp.bfloat16))
    results = lax.map(one_head, (by_head(queries), by_head(keys), by_head(values), by_head(out_grad), rand_blocks))

    def back_rows(array_in):
        return array_in.transpose(1, 2, 0, 3).reshape(NB * BS, HEADS * DH)
    return (back_rows(results[0]), back_rows(results[1]), back_rows(results[2]), back_rows(results[3]))
```

```python
import functools
import math

import jax
import jax.numpy as jnp
from jax import lax
from jax.experimental import pallas as pl
from jax.experimental.pallas import tpu as pltpu
from jax.sharding import PartitionSpec as P

KEYS, VALUES, QUERIES, GRADS, LISTS = range(5)


def flipped(index, mask):
    bit = 1
    while bit <= mask:
        if mask & bit:
            index = index + bit - 2 * bit * lax.rem(lax.div(index, bit), 2)
        bit *= 2
    return index


def kernel(
    dims,
    q_hbm, k_hbm, v_hbm, g_hbm, list_hbm,
    out_hbm, dq_hbm, dk_hbm, dv_hbm,
    qbuf, gbuf, kbuf, vbuf, ktbuf, vtbuf, obuf, dqbuf,
    dka, dva, segk, segv, redk, redv,
    list_vmem, list_smem, prev_smem, last_smem,
    in_send, in_recv, own_sem, relay_send, relay_recv,
    red_send, red_recv, ret_send, ret_recv, list_sem,
):
    groups, ranks, blks, rand, size, width = dims
    slot_count = ranks * groups * blks
    scale = 1.0 / math.sqrt(width)
    me = lax.axis_index("seq")
    group, rank = lax.div(me, ranks), lax.rem(me, ranks)
    f32, bf16 = jnp.float32, jnp.bfloat16

    def head_columns(head):
        return pl.ds(pl.multiple_of(head * width, width), width)

    def blocks(index):
        return pl.ds(index * blks, blks)

    def at_group(delta):
        return lax.rem(group + delta + groups, groups)

    def column_peer(other):
        return {"seq": other * ranks + rank}

    def row_peer(mask):
        return {"seq": group * ranks + flipped(rank, mask)}

    sources = (k_hbm, v_hbm, q_hbm, g_hbm)
    landing = (kbuf, vbuf, qbuf, gbuf)

    def scatter(which, delta):
        peer = at_group(delta)
        if which == LISTS:
            src, dst = list_hbm.at[peer], list_vmem.at[group]
        else:
            src = sources[which].at[:, :, head_columns(peer)]
            dst = landing[which].at[blocks(group)]
        if delta == 0:
            return pltpu.make_async_copy(src, dst, own_sem.at[which])
        return pltpu.make_async_remote_copy(
            src, dst, in_send.at[which, delta], in_recv.at[which, delta],
            device_id=column_peer(peer), device_id_type=pl.DeviceIdType.MESH,
        )

    def relay(which, delta, mask):
        source = at_group(-delta)
        if delta == 0:
            src = sources[which].at[:, :, head_columns(group)]
        else:
            src = landing[which].at[blocks(source)]
        return pltpu.make_async_remote_copy(
            src, landing[which].at[blocks(mask * groups + source)],
            relay_send.at[which, delta, mask], relay_recv.at[which, delta, mask],
            device_id=row_peer(mask), device_id_type=pl.DeviceIdType.MESH,
        )

    def reduce(which, step, mask):
        owner = at_group(step + 1)
        return pltpu.make_async_remote_copy(
            landing[which].at[blocks(mask * groups + owner)],
            (redk, redv)[which].at[blocks((mask - 1) * groups + owner)],
            red_send.at[which, step, mask], red_recv.at[which, step, mask],
            device_id=row_peer(mask), device_id_type=pl.DeviceIdType.MESH,
        )

    results = (dk_hbm, dv_hbm, out_hbm, dq_hbm)
    leaving = (kbuf, vbuf, obuf, dqbuf)

    def giveback(which, step, remote):
        owner = at_group(step + 1)
        src = leaving[which].at[blocks(owner)]
        dst = results[which].at[:, :, head_columns(group)]
        if not remote:
            return pltpu.make_async_copy(src, dst, ret_send.at[which, step])
        return pltpu.make_async_remote_copy(
            src, dst, ret_send.at[which, step], ret_recv.at[which, step],
            device_id=column_peer(owner), device_id_type=pl.DeviceIdType.MESH,
        )

    masks = range(1, ranks)
    deltas = range(1, groups)
    pair = (KEYS, VALUES)

    barrier = pltpu.get_barrier_semaphore()
    for delta in deltas:
        pl.semaphore_signal(
            barrier, inc=1, device_id=column_peer(at_group(delta)),
            device_id_type=pl.DeviceIdType.MESH,
        )
    for mask in masks:
        pl.semaphore_signal(
            barrier, inc=1, device_id=row_peer(mask), device_id_type=pl.DeviceIdType.MESH
        )
    pl.semaphore_wait(barrier, groups - 1 + ranks - 1)

    for delta in deltas:
        scatter(LISTS, delta).start()
    for delta in deltas:
        for which in pair:
            scatter(which, delta).start()
    for which in pair:
        for mask in masks:
            relay(which, 0, mask).start()
    for delta in deltas:
        for which in (QUERIES, GRADS):
            scatter(which, delta).start()
    for which in range(5):
        scatter(which, 0).start()

    scatter(LISTS, 0).wait()
    for delta in deltas:
        scatter(LISTS, delta).wait_recv()
    list_copy = pltpu.make_async_copy(list_vmem, list_smem, list_sem)
    list_copy.start()
    list_copy.wait()
    targets = []
    for step in range(groups):
        for lane in range(blks * rand):
            targets.append(list_smem[at_group(step + 1), 0, lane])
    for entry, target in enumerate(targets):
        found = jnp.int32(0)
        for earlier in range(entry):
            found = jnp.where(targets[earlier] == target, earlier + 1, found)
        prev_smem[entry] = found

    @pl.loop(0, slot_count)
    def _(slot):
        found = jnp.int32(0)
        for entry, target in enumerate(targets):
            found = jnp.where(target == slot, entry + 1, found)
        last_smem[slot] = found
        dka[slot] = jnp.zeros((size, width), f32)
        dva[slot] = jnp.zeros((size, width), f32)

    segk[0] = jnp.zeros((size, width), f32)
    segv[0] = jnp.zeros((size, width), f32)

    for delta in deltas:
        for which in pair:
            scatter(which, delta).wait_recv()
            for mask in masks:
                relay(which, delta, mask).start()
    for which in pair:
        scatter(which, 0).wait()

    def turn(low, high):
        @pl.loop(low, high)
        def _(slot):
            ktbuf[slot] = kbuf[slot].astype(f32).T.astype(bf16)
            vtbuf[slot] = vbuf[slot].astype(f32).T.astype(bf16)

    turn(0, groups * blks)
    for delta in range(groups):
        for which in pair:
            for mask in masks:
                relay(which, delta, mask).wait_recv()
    turn(groups * blks, slot_count)

    for which in (QUERIES, GRADS):
        scatter(which, 0).wait()
        for delta in deltas:
            scatter(which, delta).wait_recv()

    def dot(left, right, contract):
        return lax.dot_general(
            left, right, ((contract[:1], contract[1:]), ((), ())), preferred_element_type=f32
        )

    def rounded(value):
        return value.astype(bf16).astype(f32)

    def one_block(step, blk):
        owner = at_group(step + 1)
        here = owner * blks + blk
        query, grad = qbuf[here], gbuf[here]
        slots = [owner * blks + blk]
        bit = 1
        while bit < blks:
            slots.append(owner * blks + (blk ^ bit))
            bit *= 2
        bit = 1
        while bit < ranks:
            slots.append((bit * groups + owner) * blks + blk)
            bit *= 2
        bit = 1
        while bit < groups:
            slots.append(flipped(owner, bit) * blks + blk)
            bit *= 2
        fixed = len(slots)
        for pick in range(rand):
            slots.append(list_smem[owner, 0, blk * rand + pick])
        key_set = jnp.concatenate([kbuf[slot] for slot in slots], axis=0)
        value_set = jnp.concatenate([vbuf[slot] for slot in slots], axis=0)
        scores = dot(key_set, query, (1, 1)) * scale
        grad_weights = dot(value_set, grad, (1, 1))
        top = jnp.max(scores, axis=0, keepdims=True)
        raised = jnp.exp(scores - top)
        total = jnp.sum(raised, axis=0, keepdims=True)
        weights = raised * (1.0 / total)
        weights_low = weights.astype(bf16)
        value_turned = jnp.concatenate([vtbuf[slot] for slot in slots], axis=1)
        attn = rounded(dot(value_turned, weights_low, (1, 0)))
        obuf[here] = attn.T.astype(bf16)
        delta = jnp.sum(grad.astype(f32).T * attn, axis=0, keepdims=True)
        grad_scores = (weights * (grad_weights - delta)).astype(bf16)
        key_turned = jnp.concatenate([ktbuf[slot] for slot in slots], axis=1)
        dqbuf[here] = (dot(key_turned, grad_scores, (1, 0)) * scale).T.astype(bf16)
        key_terms = dot(grad_scores, query, (1, 0)) * scale
        value_terms = dot(weights_low, grad, (1, 0))
        for terms, total_ref, chain in ((key_terms, dka, segk), (value_terms, dva, segv)):
            for place, slot in enumerate(slots):
                term = terms[place * size : (place + 1) * size, :]
                if place:
                    term = rounded(term)
                if place < fixed:
                    total_ref[slot] += term
                else:
                    entry = (step * blks + blk) * rand + place - fixed
                    before = prev_smem[entry]
                    chain[entry + 1] = term + chain[before]

    @pl.loop(0, groups)
    def _(step):
        for blk in range(blks):
            one_block(step, blk)

        @pl.when(step < groups - 1)
        def _():
            for which in (2, 3):
                giveback(which, step, True).start()

        @pl.when(step == groups - 1)
        def _():
            for which in (2, 3):
                giveback(which, step, False).start()

    for delta in range(groups):
        for which in pair:
            for mask in masks:
                relay(which, delta, mask).wait_send()
    for step in range(groups):
        for which in pair:
            total_ref, chain = ((dka, segk), (dva, segv))[which]
            for mask in masks:
                first = (mask * groups + at_group(step + 1)) * blks
                for blk in range(blks):
                    here = first + blk
                    last = last_smem[here]
                    landing[which][here] = (
                        total_ref[here] + chain[last]
                    ).astype(bf16)
                reduce(which, step, mask).start()
    for step in range(groups):
        for which in pair:
            total_ref, chain = ((dka, segk), (dva, segv))[which]
            owner = at_group(step + 1)
            for mask in masks:
                reduce(which, step, mask).wait_recv()
            for blk in range(blks):
                here = owner * blks + blk
                last = last_smem[here]
                value = total_ref[here] + chain[last]
                for mask in masks:
                    there = ((mask - 1) * groups + owner) * blks + blk
                    value = value + (redk, redv)[which][there].astype(f32)
                landing[which][here] = value.astype(bf16)
            giveback(which, step, step < groups - 1).start()

    for delta in deltas:
        for which in range(5):
            scatter(which, delta).wait_send()
    for step in range(groups):
        for which in pair:
            for mask in masks:
                reduce(which, step, mask).wait_send()
        for which in (2, 3, 0, 1):
            if step < groups - 1:
                giveback(which, step, True).wait_send()
                giveback(which, step, True).wait_recv()
            else:
                giveback(which, step, False).wait()


def local(queries, keys, values, out_grad, rand_blocks):
    groups, blks, rand = rand_blocks.shape
    rows = queries.shape[0]
    size = rows // blks
    width = queries.shape[1] // groups
    ranks = lax.axis_size("seq") // groups
    slots = ranks * groups * blks
    entries = groups * blks * rand
    rank = lax.axis_index("seq") % ranks
    owner = rand_blocks // blks
    listed = (((owner % ranks) ^ rank) * groups + owner // ranks) * blks + rand_blocks % blks
    listed = listed.reshape(groups, 1, blks * rand)
    listed = jnp.pad(listed, ((0, 0), (0, 7), (0, 128 - blks * rand)))
    whole = jax.ShapeDtypeStruct((blks, size, groups * width), jnp.bfloat16)
    bf16, f32, dma = jnp.bfloat16, jnp.float32, pltpu.SemaphoreType.DMA
    flops = 12 * groups * blks * size * size * width * (rand + 1 + int(math.log2(slots)))
    arrays = [item.reshape(whole.shape) for item in (queries, keys, values, out_grad)]
    results = pl.pallas_call(
        functools.partial(kernel, (groups, ranks, blks, rand, size, width)),
        out_shape=[whole] * 4,
        in_specs=[pl.BlockSpec(memory_space=pl.ANY)] * 5,
        out_specs=[pl.BlockSpec(memory_space=pl.ANY)] * 4,
        scratch_shapes=[
            pltpu.VMEM((groups * blks, size, width), bf16),
            pltpu.VMEM((groups * blks, size, width), bf16),
            pltpu.VMEM((slots, size, width), bf16),
            pltpu.VMEM((slots, size, width), bf16),
            pltpu.VMEM((slots, width, size), bf16),
            pltpu.VMEM((slots, width, size), bf16),
            pltpu.VMEM((groups * blks, size, width), bf16),
            pltpu.VMEM((groups * blks, size, width), bf16),
            pltpu.VMEM((slots, size, width), f32),
            pltpu.VMEM((slots, size, width), f32),
            pltpu.VMEM((entries + 1, size, width), f32),
            pltpu.VMEM((entries + 1, size, width), f32),
            pltpu.VMEM(((ranks - 1) * groups * blks, size, width), bf16),
            pltpu.VMEM(((ranks - 1) * groups * blks, size, width), bf16),
            pltpu.VMEM((groups, 8, 128), jnp.int32),
            pltpu.SMEM((groups, 8, 128), jnp.int32),
            pltpu.SMEM((entries,), jnp.int32),
            pltpu.SMEM((slots,), jnp.int32),
            dma((5, groups)),
            dma((5, groups)),
            dma((5,)),
            dma((2, groups, ranks)),
            dma((2, groups, ranks)),
            dma((2, groups, ranks)),
            dma((2, groups, ranks)),
            dma((4, groups)),
            dma((4, groups)),
            dma,
        ],
        compiler_params=pltpu.CompilerParams(
            collective_id=0, has_side_effects=True, vmem_limit_bytes=56 * 2**20
        ),
        cost_estimate=pl.CostEstimate(
            flops=flops, bytes_accessed=16 * rows * groups * width, transcendentals=0
        ),
    )(*arrays, listed)
    return tuple(item.reshape(queries.shape) for item in results)


def solution(mesh):
    spec = P("seq", "head")
    return jax.shard_map(
        local,
        mesh=mesh,
        in_specs=(spec, spec, spec, spec, P("head", "seq", None)),
        out_specs=(spec, spec, spec, spec),
        check_vma=False,
    )
```

```python
import functools
import math

import jax
import jax.numpy as jnp
from jax import lax
from jax.experimental import pallas as pl
from jax.experimental.pallas import tpu as pltpu
from jax.sharding import PartitionSpec as P

KEYS, VALUES, QUERIES, GRADS, LISTS = range(5)


def flipped(index, mask):
    bit = 1
    while bit <= mask:
        if mask & bit:
            index = index + bit - 2 * bit * lax.rem(lax.div(index, bit), 2)
        bit *= 2
    return index


def kernel(
    dims,
    q_hbm, k_hbm, v_hbm, g_hbm, list_hbm,
    out_hbm, dq_hbm, dk_hbm, dv_hbm,
    qbuf, gbuf, kbuf, vbuf, ktbuf, vtbuf, obuf, dqbuf,
    dka, dva, segk, segv, redk, redv,
    list_vmem, list_smem, prev_smem, last_smem,
    in_send, in_recv, own_sem, relay_send, relay_recv,
    red_send, red_recv, ret_send, ret_recv, list_sem,
):
    groups, ranks, blks, rand, size, width = dims
    slot_count = ranks * groups * blks
    scale = 1.0 / math.sqrt(width)
    me = lax.axis_index("seq")
    group, rank = lax.div(me, ranks), lax.rem(me, ranks)
    f32, bf16 = jnp.float32, jnp.bfloat16

    def head_columns(head):
        return pl.ds(pl.multiple_of(head * width, width), width)

    def blocks(index):
        return pl.ds(index * blks, blks)

    def at_group(delta):
        return flipped(group, delta)

    def column_peer(other):
        return {"seq": other * ranks + rank}

    def row_peer(mask):
        return {"seq": group * ranks + flipped(rank, mask)}

    sources = (k_hbm, v_hbm, q_hbm, g_hbm)
    landing = (kbuf, vbuf, qbuf, gbuf)

    def scatter(which, delta):
        peer = at_group(delta)
        if which == LISTS:
            src, dst = list_hbm.at[peer], list_vmem.at[group]
        else:
            src = sources[which].at[:, :, head_columns(peer)]
            dst = landing[which].at[blocks(group)]
        if delta == 0:
            return pltpu.make_async_copy(src, dst, own_sem.at[which])
        return pltpu.make_async_remote_copy(
            src, dst, in_send.at[which, delta], in_recv.at[which, delta],
            device_id=column_peer(peer), device_id_type=pl.DeviceIdType.MESH,
        )

    def relay(which, delta, mask):
        source = at_group(delta)
        if delta == 0:
            src = sources[which].at[:, :, head_columns(group)]
        else:
            src = landing[which].at[blocks(source)]
        return pltpu.make_async_remote_copy(
            src, landing[which].at[blocks(mask * groups + source)],
            relay_send.at[which, delta, mask], relay_recv.at[which, delta, mask],
            device_id=row_peer(mask), device_id_type=pl.DeviceIdType.MESH,
        )

    def reduce(which, step, mask):
        owner = at_group(step)
        return pltpu.make_async_remote_copy(
            landing[which].at[blocks(mask * groups + owner)],
            (redk, redv)[which].at[blocks((mask - 1) * groups + owner)],
            red_send.at[which, step, mask], red_recv.at[which, step, mask],
            device_id=row_peer(mask), device_id_type=pl.DeviceIdType.MESH,
        )

    results = (dk_hbm, dv_hbm, out_hbm, dq_hbm)
    leaving = (kbuf, vbuf, obuf, dqbuf)

    def giveback(which, step):
        owner = at_group(step)
        src = leaving[which].at[blocks(owner)]
        dst = results[which].at[:, :, head_columns(group)]
        if step == 0:
            return pltpu.make_async_copy(src, dst, ret_send.at[which, step])
        return pltpu.make_async_remote_copy(
            src, dst, ret_send.at[which, step], ret_recv.at[which, step],
            device_id=column_peer(owner), device_id_type=pl.DeviceIdType.MESH,
        )

    masks = range(1, ranks)
    deltas = [*range(groups // 2, groups), *range(1, groups // 2)]
    pair = (KEYS, VALUES)

    barrier = pltpu.get_barrier_semaphore()
    for delta in deltas:
        pl.semaphore_signal(
            barrier, inc=1, device_id=column_peer(at_group(delta)),
            device_id_type=pl.DeviceIdType.MESH,
        )
    for mask in masks:
        pl.semaphore_signal(
            barrier, inc=1, device_id=row_peer(mask), device_id_type=pl.DeviceIdType.MESH
        )
    pl.semaphore_wait(barrier, groups - 1 + ranks - 1)

    for delta in deltas:
        scatter(LISTS, delta).start()
    for delta in deltas:
        for which in pair:
            scatter(which, delta).start()
    for which in pair:
        for mask in masks:
            relay(which, 0, mask).start()
    for delta in deltas:
        for which in (QUERIES, GRADS):
            scatter(which, delta).start()
    for which in range(5):
        scatter(which, 0).start()

    scatter(LISTS, 0).wait()
    for delta in deltas:
        scatter(LISTS, delta).wait_recv()
    list_copy = pltpu.make_async_copy(list_vmem, list_smem, list_sem)
    list_copy.start()
    list_copy.wait()
    targets = []
    for step in range(groups):
        for lane in range(blks * rand):
            targets.append(list_smem[at_group(step), 0, lane])
    for entry, target in enumerate(targets):
        found = jnp.int32(0)
        for earlier in range(entry):
            found = jnp.where(targets[earlier] == target, earlier + 1, found)
        prev_smem[entry] = found

    @pl.loop(0, slot_count)
    def _(slot):
        found = jnp.int32(0)
        for entry, target in enumerate(targets):
            found = jnp.where(target == slot, entry + 1, found)
        last_smem[slot] = found
        dka[slot] = jnp.zeros((size, width), f32)
        dva[slot] = jnp.zeros((size, width), f32)

    segk[0] = jnp.zeros((size, width), f32)
    segv[0] = jnp.zeros((size, width), f32)

    for delta in deltas:
        for which in pair:
            scatter(which, delta).wait_recv()
            for mask in masks:
                relay(which, delta, mask).start()
    for which in pair:
        scatter(which, 0).wait()

    def turn(low, high):
        @pl.loop(low, high)
        def _(slot):
            ktbuf[slot] = kbuf[slot].astype(f32).T.astype(bf16)
            vtbuf[slot] = vbuf[slot].astype(f32).T.astype(bf16)

    turn(0, groups * blks)
    for delta in range(groups):
        for which in pair:
            for mask in masks:
                relay(which, delta, mask).wait_recv()
    turn(groups * blks, slot_count)

    def dot(left, right, contract):
        return lax.dot_general(
            left, right, ((contract[:1], contract[1:]), ((), ())), preferred_element_type=f32
        )

    def rounded(value):
        return value.astype(bf16).astype(f32)

    def one_block(step, owner, blk):
        here = owner * blks + blk
        query, grad = qbuf[here], gbuf[here]
        slots = [owner * blks + blk]
        bit = 1
        while bit < blks:
            slots.append(owner * blks + (blk ^ bit))
            bit *= 2
        bit = 1
        while bit < ranks:
            slots.append((bit * groups + owner) * blks + blk)
            bit *= 2
        bit = 1
        while bit < groups:
            slots.append(flipped(owner, bit) * blks + blk)
            bit *= 2
        fixed = len(slots)
        for pick in range(rand):
            slots.append(list_smem[owner, 0, blk * rand + pick])
        key_set = jnp.concatenate([kbuf[slot] for slot in slots], axis=0)
        value_set = jnp.concatenate([vbuf[slot] for slot in slots], axis=0)
        scores = dot(key_set, query, (1, 1)) * scale
        grad_weights = dot(value_set, grad, (1, 1))
        top = jnp.max(scores, axis=0, keepdims=True)
        raised = jnp.exp(scores - top)
        total = jnp.sum(raised, axis=0, keepdims=True)
        weights = raised * (1.0 / total)
        weights_low = weights.astype(bf16)
        value_turned = jnp.concatenate([vtbuf[slot] for slot in slots], axis=1)
        attn = rounded(dot(value_turned, weights_low, (1, 0)))
        obuf[here] = attn.T.astype(bf16)
        delta = jnp.sum(grad.astype(f32).T * attn, axis=0, keepdims=True)
        grad_scores = (weights * (grad_weights - delta)).astype(bf16)
        key_turned = jnp.concatenate([ktbuf[slot] for slot in slots], axis=1)
        dqbuf[here] = (dot(key_turned, grad_scores, (1, 0)) * scale).T.astype(bf16)
        key_terms = dot(grad_scores, query, (1, 0)) * scale
        value_terms = dot(weights_low, grad, (1, 0))
        for terms, total_ref, chain in ((key_terms, dka, segk), (value_terms, dva, segv)):
            for place, slot in enumerate(slots):
                term = terms[place * size : (place + 1) * size, :]
                if place:
                    term = rounded(term)
                if place < fixed:
                    total_ref[slot] += term
                else:
                    entry = (step * blks + blk) * rand + place - fixed
                    before = prev_smem[entry]
                    chain[entry + 1] = term + chain[before]

    for step in range(groups):
        for which in (QUERIES, GRADS):
            if step:
                scatter(which, step).wait_recv()
            else:
                scatter(which, step).wait()
        for blk in range(blks):
            one_block(step, at_group(step), blk)
        for which in (2, 3):
            giveback(which, step).start()

    for delta in range(groups):
        for which in pair:
            for mask in masks:
                relay(which, delta, mask).wait_send()
    for step in (*deltas, 0):
        for which in pair:
            total_ref, chain = ((dka, segk), (dva, segv))[which]
            for mask in masks:
                first = (mask * groups + at_group(step)) * blks
                for blk in range(blks):
                    here = first + blk
                    last = last_smem[here]
                    landing[which][here] = (
                        total_ref[here] + chain[last]
                    ).astype(bf16)
                reduce(which, step, mask).start()
    for step in (*deltas, 0):
        for which in pair:
            total_ref, chain = ((dka, segk), (dva, segv))[which]
            owner = at_group(step)
            for mask in masks:
                reduce(which, step, mask).wait_recv()
            for blk in range(blks):
                here = owner * blks + blk
                last = last_smem[here]
                value = total_ref[here] + chain[last]
                for mask in masks:
                    there = ((mask - 1) * groups + owner) * blks + blk
                    value = value + (redk, redv)[which][there].astype(f32)
                landing[which][here] = value.astype(bf16)
            giveback(which, step).start()

    for delta in deltas:
        for which in range(5):
            scatter(which, delta).wait_send()
    for step in (*deltas, 0):
        for which in pair:
            for mask in masks:
                reduce(which, step, mask).wait_send()
        for which in (2, 3, 0, 1):
            giveback(which, step).wait()


def handed_out(*refs):
    sources, targets, sem = refs[:4], refs[4:8], refs[8]
    copies = [
        pltpu.make_async_copy(source, target, sem.at[place])
        for place, (source, target) in enumerate(zip(sources, targets))
    ]
    for copy in copies:
        copy.start()
    for copy in copies:
        copy.wait()


def local(queries, keys, values, out_grad, rand_blocks):
    groups, blks, rand = rand_blocks.shape
    rows = queries.shape[0]
    size = rows // blks
    width = queries.shape[1] // groups
    ranks = lax.axis_size("seq") // groups
    slots = ranks * groups * blks
    entries = groups * blks * rand
    rank = lax.axis_index("seq") % ranks
    owner = rand_blocks // blks
    listed = (((owner % ranks) ^ rank) * groups + owner // ranks) * blks + rand_blocks % blks
    listed = listed.reshape(groups, 1, blks * rand)
    listed = jnp.pad(listed, ((0, 0), (0, 7), (0, 128 - blks * rand)))
    whole = jax.ShapeDtypeStruct((blks, size, groups * width), jnp.bfloat16)
    bf16, f32, dma = jnp.bfloat16, jnp.float32, pltpu.SemaphoreType.DMA
    flops = 12 * groups * blks * size * size * width * (rand + 1 + int(math.log2(slots)))
    arrays = [item.reshape(whole.shape) for item in (queries, keys, values, out_grad)]
    results = pl.pallas_call(
        functools.partial(kernel, (groups, ranks, blks, rand, size, width)),
        out_shape=[whole] * 4,
        in_specs=[pl.BlockSpec(memory_space=pl.ANY)] * 5,
        out_specs=[pl.BlockSpec(memory_space=pl.ANY)] * 4,
        scratch_shapes=[
            pltpu.VMEM((groups * blks, size, width), bf16),
            pltpu.VMEM((groups * blks, size, width), bf16),
            pltpu.VMEM((slots, size, width), bf16),
            pltpu.VMEM((slots, size, width), bf16),
            pltpu.VMEM((slots, width, size), bf16),
            pltpu.VMEM((slots, width, size), bf16),
            pltpu.VMEM((groups * blks, size, width), bf16),
            pltpu.VMEM((groups * blks, size, width), bf16),
            pltpu.VMEM((slots, size, width), f32),
            pltpu.VMEM((slots, size, width), f32),
            pltpu.VMEM((entries + 1, size, width), f32),
            pltpu.VMEM((entries + 1, size, width), f32),
            pltpu.VMEM(((ranks - 1) * groups * blks, size, width), bf16),
            pltpu.VMEM(((ranks - 1) * groups * blks, size, width), bf16),
            pltpu.VMEM((groups, 8, 128), jnp.int32),
            pltpu.SMEM((groups, 8, 128), jnp.int32),
            pltpu.SMEM((entries,), jnp.int32),
            pltpu.SMEM((slots,), jnp.int32),
            dma((5, groups)),
            dma((5, groups)),
            dma((5,)),
            dma((2, groups, ranks)),
            dma((2, groups, ranks)),
            dma((2, groups, ranks)),
            dma((2, groups, ranks)),
            dma((4, groups)),
            dma((4, groups)),
            dma,
        ],
        compiler_params=pltpu.CompilerParams(
            collective_id=0, has_side_effects=True, vmem_limit_bytes=56 * 2**20
        ),
        cost_estimate=pl.CostEstimate(
            flops=flops, bytes_accessed=16 * rows * groups * width, transcendentals=0
        ),
    )(*arrays, listed)
    results = pl.pallas_call(
        handed_out,
        out_shape=[whole] * 4,
        in_specs=[pl.BlockSpec(memory_space=pl.ANY)] * 4,
        out_specs=[pl.BlockSpec(memory_space=pl.ANY)] * 4,
        scratch_shapes=[dma((4,))],
        cost_estimate=pl.CostEstimate(
            flops=0, bytes_accessed=16 * rows * groups * width, transcendentals=0
        ),
    )(*results)
    return tuple(item.reshape(queries.shape) for item in results)


def solution(mesh):
    spec = P("seq", "head")
    return jax.shard_map(
        local,
        mesh=mesh,
        in_specs=(spec, spec, spec, spec, P("head", "seq", None)),
        out_specs=(spec, spec, spec, spec),
        check_vma=False,
    )
```

```python
import functools
import math

import jax
import jax.numpy as jnp
from jax import lax
from jax.experimental import pallas as pl
from jax.experimental.pallas import tpu as pltpu
from jax.sharding import PartitionSpec as P

KEYS, VALUES, QUERIES, GRADS, LISTS = range(5)


def flipped(index, mask):
    bit = 1
    while bit <= mask:
        if mask & bit:
            index = index + bit - 2 * bit * lax.rem(lax.div(index, bit), 2)
        bit *= 2
    return index


def kernel(
    dims,
    q_hbm, k_hbm, v_hbm, g_hbm, list_hbm,
    out_hbm, dq_hbm, dk_hbm, dv_hbm,
    qbuf, gbuf, kbuf, vbuf, ktbuf, vtbuf, obuf, dqbuf,
    dka, dva, segk, segv, redk, redv,
    list_vmem, list_smem, prev_smem, last_smem,
    in_send, in_recv, own_sem, relay_send, relay_recv,
    red_send, red_recv, ret_send, ret_recv, list_sem,
):
    groups, ranks, blks, rand, size, width = dims
    slot_count = ranks * groups * blks
    scale = 1.0 / math.sqrt(width)
    me = lax.axis_index("seq")
    group, rank = lax.div(me, ranks), lax.rem(me, ranks)
    f32, bf16 = jnp.float32, jnp.bfloat16

    def head_columns(head):
        return pl.ds(pl.multiple_of(head * width, width), width)

    def blocks(index):
        return pl.ds(index * blks, blks)

    def at_group(delta):
        return lax.rem(group + delta + groups, groups)

    def column_peer(other):
        return {"seq": other * ranks + rank}

    def row_peer(mask):
        return {"seq": group * ranks + flipped(rank, mask)}

    sources = (k_hbm, v_hbm, q_hbm, g_hbm)
    landing = (kbuf, vbuf, qbuf, gbuf)

    def scatter(which, delta):
        peer = at_group(delta)
        if which == LISTS:
            src, dst = list_hbm.at[peer], list_vmem.at[group]
        else:
            src = sources[which].at[:, :, head_columns(peer)]
            dst = landing[which].at[blocks(group)]
        if delta == 0:
            return pltpu.make_async_copy(src, dst, own_sem.at[which])
        return pltpu.make_async_remote_copy(
            src, dst, in_send.at[which, delta], in_recv.at[which, delta],
            device_id=column_peer(peer), device_id_type=pl.DeviceIdType.MESH,
        )

    def relay(which, delta, mask):
        source = at_group(-delta)
        if delta == 0:
            src = sources[which].at[:, :, head_columns(group)]
        else:
            src = landing[which].at[blocks(source)]
        return pltpu.make_async_remote_copy(
            src, landing[which].at[blocks(mask * groups + source)],
            relay_send.at[which, delta, mask], relay_recv.at[which, delta, mask],
            device_id=row_peer(mask), device_id_type=pl.DeviceIdType.MESH,
        )

    def reduce(which, step, mask):
        owner = at_group(step + 1)
        return pltpu.make_async_remote_copy(
            landing[which].at[blocks(mask * groups + owner)],
            (redk, redv)[which].at[blocks((mask - 1) * groups + owner)],
            red_send.at[which, step, mask], red_recv.at[which, step, mask],
            device_id=row_peer(mask), device_id_type=pl.DeviceIdType.MESH,
        )

    results = (dk_hbm, dv_hbm, out_hbm, dq_hbm)
    leaving = (kbuf, vbuf, obuf, dqbuf)

    def giveback(which, step, remote):
        owner = at_group(step + 1)
        src = leaving[which].at[blocks(owner)]
        dst = results[which].at[:, :, head_columns(group)]
        if not remote:
            return pltpu.make_async_copy(src, dst, ret_send.at[which, step])
        return pltpu.make_async_remote_copy(
            src, dst, ret_send.at[which, step], ret_recv.at[which, step],
            device_id=column_peer(owner), device_id_type=pl.DeviceIdType.MESH,
        )

    masks = range(1, ranks)
    deltas = range(1, groups)
    pair = (KEYS, VALUES)

    barrier = pltpu.get_barrier_semaphore()
    for delta in deltas:
        pl.semaphore_signal(
            barrier, inc=1, device_id=column_peer(at_group(delta)),
            device_id_type=pl.DeviceIdType.MESH,
        )
    for mask in masks:
        pl.semaphore_signal(
            barrier, inc=1, device_id=row_peer(mask), device_id_type=pl.DeviceIdType.MESH
        )
    pl.semaphore_wait(barrier, groups - 1 + ranks - 1)

    for delta in deltas:
        scatter(LISTS, delta).start()
    for delta in deltas:
        for which in pair:
            scatter(which, delta).start()
    for which in pair:
        for mask in masks:
            relay(which, 0, mask).start()
    for delta in deltas:
        for which in (QUERIES, GRADS):
            scatter(which, delta).start()
    for which in range(5):
        scatter(which, 0).start()

    scatter(LISTS, 0).wait()
    for delta in deltas:
        scatter(LISTS, delta).wait_recv()
    list_copy = pltpu.make_async_copy(list_vmem, list_smem, list_sem)
    list_copy.start()
    list_copy.wait()
    targets = []
    for step in range(groups):
        for lane in range(blks * rand):
            targets.append(list_smem[at_group(step + 1), 0, lane])
    for entry, target in enumerate(targets):
        found = jnp.int32(0)
        for earlier in range(entry):
            found = jnp.where(targets[earlier] == target, earlier + 1, found)
        prev_smem[entry] = found

    @pl.loop(0, slot_count)
    def _(slot):
        found = jnp.int32(0)
        for entry, target in enumerate(targets):
            found = jnp.where(target == slot, entry + 1, found)
        last_smem[slot] = found
        dka[slot] = jnp.zeros((size, width), f32)
        dva[slot] = jnp.zeros((size, width), f32)

    segk[0] = jnp.zeros((size, width), f32)
    segv[0] = jnp.zeros((size, width), f32)

    for delta in deltas:
        for which in pair:
            scatter(which, delta).wait_recv()
            for mask in masks:
                relay(which, delta, mask).start()
    for which in pair:
        scatter(which, 0).wait()

    def turn(low, high):
        @pl.loop(low, high)
        def _(slot):
            ktbuf[slot] = kbuf[slot].astype(f32).T.astype(bf16)
            vtbuf[slot] = vbuf[slot].astype(f32).T.astype(bf16)

    turn(0, groups * blks)
    for delta in range(groups):
        for which in pair:
            for mask in masks:
                relay(which, delta, mask).wait_recv()
    turn(groups * blks, slot_count)

    for which in (QUERIES, GRADS):
        scatter(which, 0).wait()
        for delta in deltas:
            scatter(which, delta).wait_recv()

    def dot(left, right, contract):
        return lax.dot_general(
            left, right, ((contract[:1], contract[1:]), ((), ())), preferred_element_type=f32
        )

    def rounded(value):
        return value.astype(bf16).astype(f32)

    def one_block(step, blk):
        owner = at_group(step + 1)
        here = owner * blks + blk
        query, grad = qbuf[here], gbuf[here]
        slots = [owner * blks + blk]
        bit = 1
        while bit < blks:
            slots.append(owner * blks + (blk ^ bit))
            bit *= 2
        bit = 1
        while bit < ranks:
            slots.append((bit * groups + owner) * blks + blk)
            bit *= 2
        bit = 1
        while bit < groups:
            slots.append(flipped(owner, bit) * blks + blk)
            bit *= 2
        fixed = len(slots)
        for pick in range(rand):
            slots.append(list_smem[owner, 0, blk * rand + pick])
        key_set = jnp.concatenate([kbuf[slot] for slot in slots], axis=0)
        value_set = jnp.concatenate([vbuf[slot] for slot in slots], axis=0)
        scores = dot(key_set, query, (1, 1)) * scale
        grad_weights = dot(value_set, grad, (1, 1))
        top = jnp.max(scores, axis=0, keepdims=True)
        raised = jnp.exp(scores - top)
        total = jnp.sum(raised, axis=0, keepdims=True)
        weights = raised * (1.0 / total)
        weights_low = weights.astype(bf16)
        value_turned = jnp.concatenate([vtbuf[slot] for slot in slots], axis=1)
        attn = rounded(dot(value_turned, weights_low, (1, 0)))
        obuf[here] = attn.T.astype(bf16)
        delta = jnp.sum(grad.astype(f32).T * attn, axis=0, keepdims=True)
        grad_scores = (weights * (grad_weights - delta)).astype(bf16)
        key_turned = jnp.concatenate([ktbuf[slot] for slot in slots], axis=1)
        dqbuf[here] = (dot(key_turned, grad_scores, (1, 0)) * scale).T.astype(bf16)
        key_terms = dot(grad_scores, query, (1, 0)) * scale
        value_terms = dot(weights_low, grad, (1, 0))
        for terms, total_ref, chain in ((key_terms, dka, segk), (value_terms, dva, segv)):
            for place, slot in enumerate(slots):
                term = terms[place * size : (place + 1) * size, :]
                if place:
                    term = rounded(term)
                if place < fixed:
                    total_ref[slot] += term
                else:
                    entry = (step * blks + blk) * rand + place - fixed
                    before = prev_smem[entry]
                    chain[entry + 1] = term + chain[before]

    @pl.loop(0, groups)
    def _(step):
        for blk in range(blks):
            one_block(step, blk)

        @pl.when(step < groups - 1)
        def _():
            for which in (2, 3):
                giveback(which, step, True).start()

        @pl.when(step == groups - 1)
        def _():
            for which in (2, 3):
                giveback(which, step, False).start()

    for delta in range(groups):
        for which in pair:
            for mask in masks:
                relay(which, delta, mask).wait_send()
    for step in range(groups):
        for which in pair:
            total_ref, chain = ((dka, segk), (dva, segv))[which]
            for mask in masks:
                first = (mask * groups + at_group(step + 1)) * blks
                for blk in range(blks):
                    here = first + blk
                    last = last_smem[here]
                    landing[which][here] = (
                        total_ref[here] + chain[last]
                    ).astype(bf16)
                reduce(which, step, mask).start()
    for step in range(groups):
        for which in pair:
            total_ref, chain = ((dka, segk), (dva, segv))[which]
            owner = at_group(step + 1)
            for mask in masks:
                reduce(which, step, mask).wait_recv()
            for blk in range(blks):
                here = owner * blks + blk
                last = last_smem[here]
                value = total_ref[here] + chain[last]
                for mask in masks:
                    there = ((mask - 1) * groups + owner) * blks + blk
                    value = value + (redk, redv)[which][there].astype(f32)
                landing[which][here] = value.astype(bf16)
            giveback(which, step, step < groups - 1).start()

    for delta in deltas:
        for which in range(5):
            scatter(which, delta).wait_send()
    for step in range(groups):
        for which in pair:
            for mask in masks:
                reduce(which, step, mask).wait_send()
        for which in (2, 3, 0, 1):
            if step < groups - 1:
                giveback(which, step, True).wait_send()
                giveback(which, step, True).wait_recv()
            else:
                giveback(which, step, False).wait()


def handed_out(*refs):
    for source, target in zip(refs[:4], refs[4:]):
        target[...] = source[...]


def local(queries, keys, values, out_grad, rand_blocks):
    groups, blks, rand = rand_blocks.shape
    rows = queries.shape[0]
    size = rows // blks
    width = queries.shape[1] // groups
    ranks = lax.axis_size("seq") // groups
    slots = ranks * groups * blks
    entries = groups * blks * rand
    rank = lax.axis_index("seq") % ranks
    owner = rand_blocks // blks
    listed = (((owner % ranks) ^ rank) * groups + owner // ranks) * blks + rand_blocks % blks
    listed = listed.reshape(groups, 1, blks * rand)
    listed = jnp.pad(listed, ((0, 0), (0, 7), (0, 128 - blks * rand)))
    whole = jax.ShapeDtypeStruct((blks, size, groups * width), jnp.bfloat16)
    bf16, f32, dma = jnp.bfloat16, jnp.float32, pltpu.SemaphoreType.DMA
    flops = 12 * groups * blks * size * size * width * (rand + 1 + int(math.log2(slots)))
    arrays = [item.reshape(whole.shape) for item in (queries, keys, values, out_grad)]
    results = pl.pallas_call(
        functools.partial(kernel, (groups, ranks, blks, rand, size, width)),
        out_shape=[whole] * 4,
        in_specs=[pl.BlockSpec(memory_space=pl.ANY)] * 5,
        out_specs=[pl.BlockSpec(memory_space=pl.ANY)] * 4,
        scratch_shapes=[
            pltpu.VMEM((groups * blks, size, width), bf16),
            pltpu.VMEM((groups * blks, size, width), bf16),
            pltpu.VMEM((slots, size, width), bf16),
            pltpu.VMEM((slots, size, width), bf16),
            pltpu.VMEM((slots, width, size), bf16),
            pltpu.VMEM((slots, width, size), bf16),
            pltpu.VMEM((groups * blks, size, width), bf16),
            pltpu.VMEM((groups * blks, size, width), bf16),
            pltpu.VMEM((slots, size, width), f32),
            pltpu.VMEM((slots, size, width), f32),
            pltpu.VMEM((entries + 1, size, width), f32),
            pltpu.VMEM((entries + 1, size, width), f32),
            pltpu.VMEM(((ranks - 1) * groups * blks, size, width), bf16),
            pltpu.VMEM(((ranks - 1) * groups * blks, size, width), bf16),
            pltpu.VMEM((groups, 8, 128), jnp.int32),
            pltpu.SMEM((groups, 8, 128), jnp.int32),
            pltpu.SMEM((entries,), jnp.int32),
            pltpu.SMEM((slots,), jnp.int32),
            dma((5, groups)),
            dma((5, groups)),
            dma((5,)),
            dma((2, groups, ranks)),
            dma((2, groups, ranks)),
            dma((2, groups, ranks)),
            dma((2, groups, ranks)),
            dma((4, groups)),
            dma((4, groups)),
            dma,
        ],
        compiler_params=pltpu.CompilerParams(
            collective_id=0, has_side_effects=True, vmem_limit_bytes=56 * 2**20
        ),
        cost_estimate=pl.CostEstimate(
            flops=flops, bytes_accessed=16 * rows * groups * width, transcendentals=0
        ),
    )(*arrays, listed)
    results = pl.pallas_call(
        handed_out,
        out_shape=[whole] * 4,
        in_specs=[pl.BlockSpec(memory_space=pltpu.VMEM)] * 4,
        out_specs=[pl.BlockSpec(memory_space=pltpu.VMEM)] * 4,
        compiler_params=pltpu.CompilerParams(vmem_limit_bytes=16 * 2**20),
    )(*results)
    return tuple(item.reshape(queries.shape) for item in results)


def solution(mesh):
    spec = P("seq", "head")
    return jax.shard_map(
        local,
        mesh=mesh,
        in_specs=(spec, spec, spec, spec, P("head", "seq", None)),
        out_specs=(spec, spec, spec, spec),
        check_vma=False,
    )
```

```python
import functools
import math

import jax
import jax.numpy as jnp
from jax import lax
from jax.experimental import pallas as pl
from jax.experimental.pallas import tpu as pltpu
from jax.sharding import PartitionSpec as P

KEYS, VALUES, QUERIES, GRADS, LISTS = range(5)


def flipped(index, mask):
    bit = 1
    while bit <= mask:
        if mask & bit:
            index = index + bit - 2 * bit * lax.rem(lax.div(index, bit), 2)
        bit *= 2
    return index


def kernel(
    dims,
    q_hbm, k_hbm, v_hbm, g_hbm, list_hbm,
    out_hbm, dq_hbm, dk_hbm, dv_hbm,
    qbuf, gbuf, kbuf, vbuf, ktbuf, vtbuf, obuf, dqbuf,
    dka, dva, segk, segv, redk, redv,
    list_vmem, list_smem, prev_smem, last_smem,
    in_send, in_recv, own_sem, relay_send, relay_recv,
    red_send, red_recv, ret_send, ret_recv, list_sem,
):
    groups, ranks, blks, rand, size, width = dims
    slot_count = ranks * groups * blks
    scale = 1.0 / math.sqrt(width)
    me = lax.axis_index("seq")
    group, rank = lax.div(me, ranks), lax.rem(me, ranks)
    f32, bf16 = jnp.float32, jnp.bfloat16

    def head_columns(head):
        return pl.ds(pl.multiple_of(head * width, width), width)

    def blocks(index):
        return pl.ds(index * blks, blks)

    def at_group(delta):
        return lax.rem(group + delta + groups, groups)

    def column_peer(other):
        return {"seq": other * ranks + rank}

    def row_peer(mask):
        return {"seq": group * ranks + flipped(rank, mask)}

    sources = (k_hbm, v_hbm, q_hbm, g_hbm)
    landing = (kbuf, vbuf, qbuf, gbuf)

    def scatter(which, delta):
        peer = at_group(delta)
        if which == LISTS:
            src, dst = list_hbm.at[peer], list_vmem.at[group]
        else:
            src = sources[which].at[:, :, head_columns(peer)]
            dst = landing[which].at[blocks(group)]
        if isinstance(delta, int) and delta == 0:
            return pltpu.make_async_copy(src, dst, own_sem.at[which])
        return pltpu.make_async_remote_copy(
            src, dst, in_send.at[which, delta], in_recv.at[which, delta],
            device_id=column_peer(peer), device_id_type=pl.DeviceIdType.MESH,
        )

    def relay(which, delta, mask):
        source = at_group(-delta)
        if delta == 0:
            src = sources[which].at[:, :, head_columns(group)]
        else:
            src = landing[which].at[blocks(source)]
        return pltpu.make_async_remote_copy(
            src, landing[which].at[blocks(mask * groups + source)],
            relay_send.at[which, delta, mask], relay_recv.at[which, delta, mask],
            device_id=row_peer(mask), device_id_type=pl.DeviceIdType.MESH,
        )

    def reduce(which, step, mask):
        owner = at_group(-step)
        return pltpu.make_async_remote_copy(
            landing[which].at[blocks(mask * groups + owner)],
            (redk, redv)[which].at[blocks((mask - 1) * groups + owner)],
            red_send.at[which, step, mask], red_recv.at[which, step, mask],
            device_id=row_peer(mask), device_id_type=pl.DeviceIdType.MESH,
        )

    results = (dk_hbm, dv_hbm, out_hbm, dq_hbm)
    leaving = (kbuf, vbuf, obuf, dqbuf)

    def giveback(which, step, remote):
        owner = at_group(-step)
        src = leaving[which].at[blocks(owner)]
        dst = results[which].at[:, :, head_columns(group)]
        if not remote:
            return pltpu.make_async_copy(src, dst, ret_send.at[which, step])
        return pltpu.make_async_remote_copy(
            src, dst, ret_send.at[which, step], ret_recv.at[which, step],
            device_id=column_peer(owner), device_id_type=pl.DeviceIdType.MESH,
        )

    masks = range(1, ranks)
    deltas = range(1, groups)
    pair = (KEYS, VALUES)

    barrier = pltpu.get_barrier_semaphore()
    for delta in deltas:
        pl.semaphore_signal(
            barrier, inc=1, device_id=column_peer(at_group(delta)),
            device_id_type=pl.DeviceIdType.MESH,
        )
    for mask in masks:
        pl.semaphore_signal(
            barrier, inc=1, device_id=row_peer(mask), device_id_type=pl.DeviceIdType.MESH
        )
    pl.semaphore_wait(barrier, groups - 1 + ranks - 1)

    for delta in deltas:
        scatter(LISTS, delta).start()
    for delta in deltas:
        for which in pair:
            scatter(which, delta).start()
    for which in pair:
        for mask in masks:
            relay(which, 0, mask).start()
    for which in range(5):
        scatter(which, 0).start()

    scatter(LISTS, 0).wait()
    for delta in deltas:
        scatter(LISTS, delta).wait_recv()
    list_copy = pltpu.make_async_copy(list_vmem, list_smem, list_sem)
    list_copy.start()
    list_copy.wait()
    targets = []
    for step in range(groups):
        for lane in range(blks * rand):
            targets.append(list_smem[at_group(-step), 0, lane])
    for entry, target in enumerate(targets):
        found = jnp.int32(0)
        for earlier in range(entry):
            found = jnp.where(targets[earlier] == target, earlier + 1, found)
        prev_smem[entry] = found

    @pl.loop(0, slot_count)
    def _(slot):
        found = jnp.int32(0)
        for entry, target in enumerate(targets):
            found = jnp.where(target == slot, entry + 1, found)
        last_smem[slot] = found
        dka[slot] = jnp.zeros((size, width), f32)
        dva[slot] = jnp.zeros((size, width), f32)

    segk[0] = jnp.zeros((size, width), f32)
    segv[0] = jnp.zeros((size, width), f32)

    for delta in deltas:
        for which in pair:
            scatter(which, delta).wait_recv()
            for mask in masks:
                relay(which, delta, mask).start()
        for which in pair:
            scatter(which, delta).wait_send()
        for which in (QUERIES, GRADS):
            scatter(which, delta).start()
    for which in pair:
        scatter(which, 0).wait()

    def turn(low, high):
        @pl.loop(low, high)
        def _(slot):
            ktbuf[slot] = kbuf[slot].astype(f32).T.astype(bf16)
            vtbuf[slot] = vbuf[slot].astype(f32).T.astype(bf16)

    turn(0, groups * blks)
    for delta in range(groups):
        for which in pair:
            for mask in masks:
                relay(which, delta, mask).wait_recv()
    turn(groups * blks, slot_count)

    for which in (QUERIES, GRADS):
        scatter(which, 0).wait()

    def dot(left, right, contract):
        return lax.dot_general(
            left, right, ((contract[:1], contract[1:]), ((), ())), preferred_element_type=f32
        )

    def rounded(value):
        return value.astype(bf16).astype(f32)

    def one_block(step, blk):
        owner = at_group(-step)
        here = owner * blks + blk
        query, grad = qbuf[here], gbuf[here]
        slots = [owner * blks + blk]
        bit = 1
        while bit < blks:
            slots.append(owner * blks + (blk ^ bit))
            bit *= 2
        bit = 1
        while bit < ranks:
            slots.append((bit * groups + owner) * blks + blk)
            bit *= 2
        bit = 1
        while bit < groups:
            slots.append(flipped(owner, bit) * blks + blk)
            bit *= 2
        fixed = len(slots)
        for pick in range(rand):
            slots.append(list_smem[owner, 0, blk * rand + pick])
        key_set = jnp.concatenate([kbuf[slot] for slot in slots], axis=0)
        value_set = jnp.concatenate([vbuf[slot] for slot in slots], axis=0)
        scores = dot(key_set, query, (1, 1)) * scale
        grad_weights = dot(value_set, grad, (1, 1))
        top = jnp.max(scores, axis=0, keepdims=True)
        raised = jnp.exp(scores - top)
        total = jnp.sum(raised, axis=0, keepdims=True)
        weights = raised * (1.0 / total)
        weights_low = weights.astype(bf16)
        value_turned = jnp.concatenate([vtbuf[slot] for slot in slots], axis=1)
        attn = rounded(dot(value_turned, weights_low, (1, 0)))
        obuf[here] = attn.T.astype(bf16)
        delta = jnp.sum(grad.astype(f32).T * attn, axis=0, keepdims=True)
        grad_scores = (weights * (grad_weights - delta)).astype(bf16)
        key_turned = jnp.concatenate([ktbuf[slot] for slot in slots], axis=1)
        dqbuf[here] = (dot(key_turned, grad_scores, (1, 0)) * scale).T.astype(bf16)
        key_terms = dot(grad_scores, query, (1, 0)) * scale
        value_terms = dot(weights_low, grad, (1, 0))
        for terms, total_ref, chain in ((key_terms, dka, segk), (value_terms, dva, segv)):
            for place, slot in enumerate(slots):
                term = terms[place * size : (place + 1) * size, :]
                if place:
                    term = rounded(term)
                if place < fixed:
                    total_ref[slot] += term
                else:
                    entry = (step * blks + blk) * rand + place - fixed
                    before = prev_smem[entry]
                    chain[entry + 1] = term + chain[before]

    @pl.loop(0, groups)
    def _(step):
        @pl.when(step > 0)
        def _():
            for which in (QUERIES, GRADS):
                scatter(which, step).wait_recv()

        for blk in range(blks):
            one_block(step, blk)

        @pl.when(step > 0)
        def _():
            for which in (2, 3):
                giveback(which, step, True).start()

        @pl.when(step == 0)
        def _():
            for which in (2, 3):
                giveback(which, step, False).start()

    for delta in range(groups):
        for which in pair:
            for mask in masks:
                relay(which, delta, mask).wait_send()
    for step in (*deltas, 0):
        for which in pair:
            total_ref, chain = ((dka, segk), (dva, segv))[which]
            for mask in masks:
                first = (mask * groups + at_group(-step)) * blks
                for blk in range(blks):
                    here = first + blk
                    last = last_smem[here]
                    landing[which][here] = (
                        total_ref[here] + chain[last]
                    ).astype(bf16)
                reduce(which, step, mask).start()
    for step in (*deltas, 0):
        for which in pair:
            total_ref, chain = ((dka, segk), (dva, segv))[which]
            owner = at_group(-step)
            for mask in masks:
                reduce(which, step, mask).wait_recv()
            for blk in range(blks):
                here = owner * blks + blk
                last = last_smem[here]
                value = total_ref[here] + chain[last]
                for mask in masks:
                    there = ((mask - 1) * groups + owner) * blks + blk
                    value = value + (redk, redv)[which][there].astype(f32)
                landing[which][here] = value.astype(bf16)
            giveback(which, step, step > 0).start()

    for delta in deltas:
        for which in (LISTS, QUERIES, GRADS):
            scatter(which, delta).wait_send()
    for step in (*deltas, 0):
        for which in pair:
            for mask in masks:
                reduce(which, step, mask).wait_send()
        for which in (2, 3, 0, 1):
            if step > 0:
                giveback(which, step, True).wait_send()
                giveback(which, step, True).wait_recv()
            else:
                giveback(which, step, False).wait()


def local(queries, keys, values, out_grad, rand_blocks):
    groups, blks, rand = rand_blocks.shape
    rows = queries.shape[0]
    size = rows // blks
    width = queries.shape[1] // groups
    ranks = lax.axis_size("seq") // groups
    slots = ranks * groups * blks
    entries = groups * blks * rand
    rank = lax.axis_index("seq") % ranks
    owner = rand_blocks // blks
    listed = (((owner % ranks) ^ rank) * groups + owner // ranks) * blks + rand_blocks % blks
    listed = listed.reshape(groups, 1, blks * rand)
    listed = jnp.pad(listed, ((0, 0), (0, 7), (0, 128 - blks * rand)))
    whole = jax.ShapeDtypeStruct((blks, size, groups * width), jnp.bfloat16)
    bf16, f32, dma = jnp.bfloat16, jnp.float32, pltpu.SemaphoreType.DMA
    flops = 12 * groups * blks * size * size * width * (rand + 1 + int(math.log2(slots)))
    arrays = [item.reshape(whole.shape) for item in (queries, keys, values, out_grad)]
    results = pl.pallas_call(
        functools.partial(kernel, (groups, ranks, blks, rand, size, width)),
        out_shape=[whole] * 4,
        in_specs=[pl.BlockSpec(memory_space=pl.ANY)] * 5,
        out_specs=[pl.BlockSpec(memory_space=pl.ANY)] * 4,
        scratch_shapes=[
            pltpu.VMEM((groups * blks, size, width), bf16),
            pltpu.VMEM((groups * blks, size, width), bf16),
            pltpu.VMEM((slots, size, width), bf16),
            pltpu.VMEM((slots, size, width), bf16),
            pltpu.VMEM((slots, width, size), bf16),
            pltpu.VMEM((slots, width, size), bf16),
            pltpu.VMEM((groups * blks, size, width), bf16),
            pltpu.VMEM((groups * blks, size, width), bf16),
            pltpu.VMEM((slots, size, width), f32),
            pltpu.VMEM((slots, size, width), f32),
            pltpu.VMEM((entries + 1, size, width), f32),
            pltpu.VMEM((entries + 1, size, width), f32),
            pltpu.VMEM(((ranks - 1) * groups * blks, size, width), bf16),
            pltpu.VMEM(((ranks - 1) * groups * blks, size, width), bf16),
            pltpu.VMEM((groups, 8, 128), jnp.int32),
            pltpu.SMEM((groups, 8, 128), jnp.int32),
            pltpu.SMEM((entries,), jnp.int32),
            pltpu.SMEM((slots,), jnp.int32),
            dma((5, groups)),
            dma((5, groups)),
            dma((5,)),
            dma((2, groups, ranks)),
            dma((2, groups, ranks)),
            dma((2, groups, ranks)),
            dma((2, groups, ranks)),
            dma((4, groups)),
            dma((4, groups)),
            dma,
        ],
        compiler_params=pltpu.CompilerParams(
            collective_id=0, has_side_effects=True, vmem_limit_bytes=56 * 2**20
        ),
        cost_estimate=pl.CostEstimate(
            flops=flops, bytes_accessed=16 * rows * groups * width, transcendentals=0
        ),
    )(*arrays, listed)
    return tuple(item.reshape(queries.shape) for item in results)


def solution(mesh):
    spec = P("seq", "head")
    return jax.shard_map(
        local,
        mesh=mesh,
        in_specs=(spec, spec, spec, spec, P("head", "seq", None)),
        out_specs=(spec, spec, spec, spec),
        check_vma=False,
    )
```

```python
import functools
import math

import jax
import jax.numpy as jnp
from jax import lax
from jax.experimental import pallas as pl
from jax.experimental.pallas import tpu as pltpu
from jax.sharding import PartitionSpec as P

KEYS, VALUES, QUERIES, GRADS, LISTS = range(5)


def flipped(index, mask):
    bit = 1
    while bit <= mask:
        if mask & bit:
            index = index + bit - 2 * bit * lax.rem(lax.div(index, bit), 2)
        bit *= 2
    return index


def kernel(
    dims,
    q_hbm, k_hbm, v_hbm, g_hbm, list_hbm,
    out_hbm, dq_hbm, dk_hbm, dv_hbm,
    qbuf, gbuf, kbuf, vbuf, ktbuf, vtbuf, obuf, dqbuf,
    dka, dva, segk, segv, redk, redv,
    list_vmem, list_smem, prev_smem, last_smem,
    in_send, in_recv, own_sem, relay_send, relay_recv,
    red_send, red_recv, ret_send, ret_recv, list_sem,
):
    groups, ranks, blks, rand, size, width = dims
    slot_count = ranks * groups * blks
    scale = 1.0 / math.sqrt(width)
    me = lax.axis_index("seq")
    group, rank = lax.div(me, ranks), lax.rem(me, ranks)
    f32, bf16 = jnp.float32, jnp.bfloat16

    def head_columns(head):
        return pl.ds(pl.multiple_of(head * width, width), width)

    def blocks(index):
        return pl.ds(index * blks, blks)

    def at_group(delta):
        return lax.rem(group + delta + groups, groups)

    def column_peer(other):
        return {"seq": other * ranks + rank}

    def row_peer(mask):
        return {"seq": group * ranks + flipped(rank, mask)}

    sources = (k_hbm, v_hbm, q_hbm, g_hbm)
    landing = (kbuf, vbuf, qbuf, gbuf)

    def scatter(which, delta):
        peer = at_group(delta)
        if which == LISTS:
            src, dst = list_hbm.at[peer], list_vmem.at[group]
        else:
            src = sources[which].at[:, :, head_columns(peer)]
            dst = landing[which].at[blocks(group)]
        if isinstance(delta, int) and delta == 0:
            return pltpu.make_async_copy(src, dst, own_sem.at[which])
        return pltpu.make_async_remote_copy(
            src, dst, in_send.at[which, delta], in_recv.at[which, delta],
            device_id=column_peer(peer), device_id_type=pl.DeviceIdType.MESH,
        )

    def relay(which, delta, mask):
        source = at_group(-delta)
        if delta == 0:
            src = sources[which].at[:, :, head_columns(group)]
        else:
            src = landing[which].at[blocks(source)]
        return pltpu.make_async_remote_copy(
            src, landing[which].at[blocks(mask * groups + source)],
            relay_send.at[which, delta, mask], relay_recv.at[which, delta, mask],
            device_id=row_peer(mask), device_id_type=pl.DeviceIdType.MESH,
        )

    def reduce(which, step, mask):
        owner = at_group(-step)
        return pltpu.make_async_remote_copy(
            landing[which].at[blocks(mask * groups + owner)],
            (redk, redv)[which].at[blocks((mask - 1) * groups + owner)],
            red_send.at[which, step, mask], red_recv.at[which, step, mask],
            device_id=row_peer(mask), device_id_type=pl.DeviceIdType.MESH,
        )

    results = (dk_hbm, dv_hbm, out_hbm, dq_hbm)
    leaving = (kbuf, vbuf, obuf, dqbuf)

    def giveback(which, step, remote):
        owner = at_group(-step)
        src = leaving[which].at[blocks(owner)]
        dst = results[which].at[:, :, head_columns(group)]
        if not remote:
            return pltpu.make_async_copy(src, dst, ret_send.at[which, step])
        return pltpu.make_async_remote_copy(
            src, dst, ret_send.at[which, step], ret_recv.at[which, step],
            device_id=column_peer(owner), device_id_type=pl.DeviceIdType.MESH,
        )

    masks = range(1, ranks)
    deltas = [(turn % 2) * (groups // 2) + turn // 2 for turn in range(1, groups)]
    pair = (KEYS, VALUES)

    barrier = pltpu.get_barrier_semaphore()
    for delta in deltas:
        pl.semaphore_signal(
            barrier, inc=1, device_id=column_peer(at_group(delta)),
            device_id_type=pl.DeviceIdType.MESH,
        )
    for mask in masks:
        pl.semaphore_signal(
            barrier, inc=1, device_id=row_peer(mask), device_id_type=pl.DeviceIdType.MESH
        )
    pl.semaphore_wait(barrier, groups - 1 + ranks - 1)

    for delta in deltas:
        scatter(LISTS, delta).start()
    for delta in deltas:
        for which in pair:
            scatter(which, delta).start()
    for which in pair:
        for mask in masks:
            relay(which, 0, mask).start()
    for which in range(5):
        scatter(which, 0).start()

    scatter(LISTS, 0).wait()
    for delta in deltas:
        scatter(LISTS, delta).wait_recv()
    list_copy = pltpu.make_async_copy(list_vmem, list_smem, list_sem)
    list_copy.start()
    list_copy.wait()
    targets = []
    for step in (0, *deltas):
        for lane in range(blks * rand):
            targets.append(list_smem[at_group(-step), 0, lane])
    for entry, target in enumerate(targets):
        found = jnp.int32(0)
        for earlier in range(entry):
            found = jnp.where(targets[earlier] == target, earlier + 1, found)
        prev_smem[entry] = found

    @pl.loop(0, slot_count)
    def _(slot):
        found = jnp.int32(0)
        for entry, target in enumerate(targets):
            found = jnp.where(target == slot, entry + 1, found)
        last_smem[slot] = found
        dka[slot] = jnp.zeros((size, width), f32)
        dva[slot] = jnp.zeros((size, width), f32)

    segk[0] = jnp.zeros((size, width), f32)
    segv[0] = jnp.zeros((size, width), f32)

    for delta in deltas:
        for which in pair:
            scatter(which, delta).wait_recv()
            for mask in masks:
                relay(which, delta, mask).start()
        for which in pair:
            scatter(which, delta).wait_send()
        for which in (QUERIES, GRADS):
            scatter(which, delta).start()
    for which in pair:
        scatter(which, 0).wait()

    def turn(low, high):
        @pl.loop(low, high)
        def _(slot):
            ktbuf[slot] = kbuf[slot].astype(f32).T.astype(bf16)
            vtbuf[slot] = vbuf[slot].astype(f32).T.astype(bf16)

    turn(0, groups * blks)
    for delta in range(groups):
        for which in pair:
            for mask in masks:
                relay(which, delta, mask).wait_recv()
    turn(groups * blks, slot_count)

    for which in (QUERIES, GRADS):
        scatter(which, 0).wait()

    def dot(left, right, contract):
        return lax.dot_general(
            left, right, ((contract[:1], contract[1:]), ((), ())), preferred_element_type=f32
        )

    def rounded(value):
        return value.astype(bf16).astype(f32)

    def one_block(order, step, blk):
        owner = at_group(-step)
        here = owner * blks + blk
        query, grad = qbuf[here], gbuf[here]
        slots = [owner * blks + blk]
        bit = 1
        while bit < blks:
            slots.append(owner * blks + (blk ^ bit))
            bit *= 2
        bit = 1
        while bit < ranks:
            slots.append((bit * groups + owner) * blks + blk)
            bit *= 2
        bit = 1
        while bit < groups:
            slots.append(flipped(owner, bit) * blks + blk)
            bit *= 2
        fixed = len(slots)
        for pick in range(rand):
            slots.append(list_smem[owner, 0, blk * rand + pick])
        key_set = jnp.concatenate([kbuf[slot] for slot in slots], axis=0)
        value_set = jnp.concatenate([vbuf[slot] for slot in slots], axis=0)
        scores = dot(key_set, query, (1, 1)) * scale
        grad_weights = dot(value_set, grad, (1, 1))
        top = jnp.max(scores, axis=0, keepdims=True)
        raised = jnp.exp(scores - top)
        total = jnp.sum(raised, axis=0, keepdims=True)
        weights = raised * (1.0 / total)
        weights_low = weights.astype(bf16)
        value_turned = jnp.concatenate([vtbuf[slot] for slot in slots], axis=1)
        attn = rounded(dot(value_turned, weights_low, (1, 0)))
        obuf[here] = attn.T.astype(bf16)
        delta = jnp.sum(grad.astype(f32).T * attn, axis=0, keepdims=True)
        grad_scores = (weights * (grad_weights - delta)).astype(bf16)
        key_turned = jnp.concatenate([ktbuf[slot] for slot in slots], axis=1)
        dqbuf[here] = (dot(key_turned, grad_scores, (1, 0)) * scale).T.astype(bf16)
        key_terms = dot(grad_scores, query, (1, 0)) * scale
        value_terms = dot(weights_low, grad, (1, 0))
        for terms, total_ref, chain in ((key_terms, dka, segk), (value_terms, dva, segv)):
            for place, slot in enumerate(slots):
                term = terms[place * size : (place + 1) * size, :]
                if place:
                    term = rounded(term)
                if place < fixed:
                    total_ref[slot] += term
                else:
                    entry = (order * blks + blk) * rand + place - fixed
                    before = prev_smem[entry]
                    chain[entry + 1] = term + chain[before]

    @pl.loop(0, groups)
    def _(order):
        step = lax.rem(order, 2) * (groups // 2) + lax.div(order, 2)

        @pl.when(step > 0)
        def _():
            for which in (QUERIES, GRADS):
                scatter(which, step).wait_recv()

        for blk in range(blks):
            one_block(order, step, blk)

        @pl.when(step > 0)
        def _():
            for which in (2, 3):
                giveback(which, step, True).start()

        @pl.when(step == 0)
        def _():
            for which in (2, 3):
                giveback(which, step, False).start()

    for delta in range(groups):
        for which in pair:
            for mask in masks:
                relay(which, delta, mask).wait_send()
    for step in (*deltas, 0):
        for which in pair:
            total_ref, chain = ((dka, segk), (dva, segv))[which]
            for mask in masks:
                first = (mask * groups + at_group(-step)) * blks
                for blk in range(blks):
                    here = first + blk
                    last = last_smem[here]
                    landing[which][here] = (
                        total_ref[here] + chain[last]
                    ).astype(bf16)
                reduce(which, step, mask).start()
    for step in (*deltas, 0):
        for which in pair:
            total_ref, chain = ((dka, segk), (dva, segv))[which]
            owner = at_group(-step)
            for mask in masks:
                reduce(which, step, mask).wait_recv()
            for blk in range(blks):
                here = owner * blks + blk
                last = last_smem[here]
                value = total_ref[here] + chain[last]
                for mask in masks:
                    there = ((mask - 1) * groups + owner) * blks + blk
                    value = value + (redk, redv)[which][there].astype(f32)
                landing[which][here] = value.astype(bf16)
            giveback(which, step, step > 0).start()

    for delta in deltas:
        for which in (LISTS, QUERIES, GRADS):
            scatter(which, delta).wait_send()
    for step in (*deltas, 0):
        for which in pair:
            for mask in masks:
                reduce(which, step, mask).wait_send()
        for which in (2, 3, 0, 1):
            if step > 0:
                giveback(which, step, True).wait_send()
                giveback(which, step, True).wait_recv()
            else:
                giveback(which, step, False).wait()


def local(queries, keys, values, out_grad, rand_blocks):
    groups, blks, rand = rand_blocks.shape
    rows = queries.shape[0]
    size = rows // blks
    width = queries.shape[1] // groups
    ranks = lax.axis_size("seq") // groups
    slots = ranks * groups * blks
    entries = groups * blks * rand
    rank = lax.axis_index("seq") % ranks
    owner = rand_blocks // blks
    listed = (((owner % ranks) ^ rank) * groups + owner // ranks) * blks + rand_blocks % blks
    listed = listed.reshape(groups, 1, blks * rand)
    listed = jnp.pad(listed, ((0, 0), (0, 7), (0, 128 - blks * rand)))
    whole = jax.ShapeDtypeStruct((blks, size, groups * width), jnp.bfloat16)
    bf16, f32, dma = jnp.bfloat16, jnp.float32, pltpu.SemaphoreType.DMA
    flops = 12 * groups * blks * size * size * width * (rand + 1 + int(math.log2(slots)))
    arrays = [item.reshape(whole.shape) for item in (queries, keys, values, out_grad)]
    results = pl.pallas_call(
        functools.partial(kernel, (groups, ranks, blks, rand, size, width)),
        out_shape=[whole] * 4,
        in_specs=[pl.BlockSpec(memory_space=pl.ANY)] * 5,
        out_specs=[pl.BlockSpec(memory_space=pl.ANY)] * 4,
        scratch_shapes=[
            pltpu.VMEM((groups * blks, size, width), bf16),
            pltpu.VMEM((groups * blks, size, width), bf16),
            pltpu.VMEM((slots, size, width), bf16),
            pltpu.VMEM((slots, size, width), bf16),
            pltpu.VMEM((slots, width, size), bf16),
            pltpu.VMEM((slots, width, size), bf16),
            pltpu.VMEM((groups * blks, size, width), bf16),
            pltpu.VMEM((groups * blks, size, width), bf16),
            pltpu.VMEM((slots, size, width), f32),
            pltpu.VMEM((slots, size, width), f32),
            pltpu.VMEM((entries + 1, size, width), f32),
            pltpu.VMEM((entries + 1, size, width), f32),
            pltpu.VMEM(((ranks - 1) * groups * blks, size, width), bf16),
            pltpu.VMEM(((ranks - 1) * groups * blks, size, width), bf16),
            pltpu.VMEM((groups, 8, 128), jnp.int32),
            pltpu.SMEM((groups, 8, 128), jnp.int32),
            pltpu.SMEM((entries,), jnp.int32),
            pltpu.SMEM((slots,), jnp.int32),
            dma((5, groups)),
            dma((5, groups)),
            dma((5,)),
            dma((2, groups, ranks)),
            dma((2, groups, ranks)),
            dma((2, groups, ranks)),
            dma((2, groups, ranks)),
            dma((4, groups)),
            dma((4, groups)),
            dma,
        ],
        compiler_params=pltpu.CompilerParams(
            collective_id=0, has_side_effects=True, vmem_limit_bytes=56 * 2**20
        ),
        cost_estimate=pl.CostEstimate(
            flops=flops, bytes_accessed=16 * rows * groups * width, transcendentals=0
        ),
    )(*arrays, listed)
    return tuple(item.reshape(queries.shape) for item in results)


def solution(mesh):
    spec = P("seq", "head")
    return jax.shard_map(
        local,
        mesh=mesh,
        in_specs=(spec, spec, spec, spec, P("head", "seq", None)),
        out_specs=(spec, spec, spec, spec),
        check_vma=False,
    )
```
